256 devices in a mesh: section: 4 (over z_lo), dp: 16 (over z_hi, y, core), tensor: 4 (over x).
Axes of the slice: x: 4, y: 4, z: 8 (z_hi: 2, z_lo: 4; z = z_hi * 4 + z_lo), core: 2. Of those that a mesh axis runs over, the one named last changes fastest.
Arguments:
- tokens: bfloat16 [2048, 4096], P('dp', 'tensor'), may hold values from -6 to 6
- weight: bfloat16 [4, 4096, 4096], P('section', 'tensor', 'dp'), may hold values from -0.09375 to 0.09375
- out_grad: bfloat16 [2048, 4096], P('dp', 'tensor'), may hold values from -6 to 6
- owner_index: int32 [4], P('section'), may hold values from 0 to 15
- input_factor: float32 [4, 16, 4096, 1024], P('section', 'dp', 'tensor'), may hold values from -10 to 10
- output_factor: float32 [4, 4096, 1024], P('section', 'dp'), may hold values from -10 to 10
Outputs:
- preconditioned: float32 [4, 4096, 4096], P('section', 'tensor', 'dp')
The draws below stay inside these ranges and needn't reach their ends.
All inputs are finite; a program needn't handle non-finite values.
Results may differ from the reference program's by a relative error of at most 0.038.
Values may be sent and summed in bfloat16 or wider, within the bound.
No kernel may reach another device: no remote copies, remote signals or barrier semaphores. Data moves between devices by JAX's collectives and lax.ppermute only.
A program may use at most 128 MiB of HBM per device.

```python
import math
import jax
import jax.numpy as jnp
from jax import lax

WIDTH = 4096
BLOCK = 1024
OUT_BLOCK = 1024
TOK_DEV = 128
SECTIONS = 4
REPLICAS = 16
TOKENS = 2048


def build_blocks(key, noise, size):
    diagonal = jnp.exp(jax.random.uniform(key, noise.shape[:-1], jnp.float32, 0.0, math.log(8.0)))
    root = jnp.sqrt(diagonal)
    paired = (noise + jnp.swapaxes(noise, -1, -2)) * (0.4 / math.sqrt(2.0 * size))
    spread = paired * root[..., :, None] * root[..., None, :]
    identity = jnp.eye(size, dtype=jnp.float32)
    return spread * (1.0 - identity) + identity * diagonal[..., :, None]


def draw_input_factor(key, part):
    key = jax.random.fold_in(key, 11)
    diag_key, noise_key = jax.random.split(key)
    shape = (SECTIONS, REPLICAS, WIDTH // BLOCK, BLOCK, BLOCK)
    noise = jnp.clip(jax.random.normal(noise_key, shape, jnp.float32), -4.0, 4.0)
    blocks = build_blocks(diag_key, noise, BLOCK)
    return blocks.reshape(SECTIONS, REPLICAS, WIDTH, BLOCK)


def draw_output_factor(key, part):
    key = jax.random.fold_in(key, 12)
    diag_key, noise_key = jax.random.split(key)
    shape = (SECTIONS, WIDTH // OUT_BLOCK, OUT_BLOCK, OUT_BLOCK)
    noise = jnp.clip(jax.random.normal(noise_key, shape, jnp.float32), -4.0, 4.0)
    blocks = build_blocks(diag_key, noise, OUT_BLOCK)
    return blocks.reshape(SECTIONS, WIDTH, OUT_BLOCK)


def plant(entries, rng, low, largest):
    longest = entries.shape.index(max(entries.shape))
    spots = []
    for shift in (0, 1):
        where = [jax.random.randint(jax.random.fold_in(rng, axis), (), 0, length) for axis, length in enumerate(entries.shape)]
        where[longest] = (where[longest] + shift) % entries.shape[longest]
        spots.append(tuple(where))
    return entries.at[spots[0]].set(low).at[spots[1]].set(largest)


def level_of(key, dims, shards, smallest, top_value):
    def one(axis_at, parts):
        heights = jax.random.uniform(jax.random.fold_in(jax.random.fold_in(key, 6), axis_at), (parts,), jnp.float32, smallest / len(shards), top_value / len(shards))
        return jnp.repeat(jnp.exp(heights), dims[axis_at] // parts).reshape((-1,) + (1,) * (len(dims) - axis_at - 1))

    factor_of = one(*shards[0])
    for cut in shards[1:]:
        factor_of = factor_of * one(*cut)
    return factor_of


def normal_values(stream_key, extent, scale, limit, cuts=(), kind=jnp.bfloat16):
    drawn = jax.random.normal(stream_key, extent, jnp.float32) * scale
    if len(cuts) > 0:
        drawn = level_of(stream_key, extent, cuts, -0.22, 0.18) * drawn
    return jnp.clip(drawn, min=-limit, max=limit).astype(kind)


def setup_inputs(seed: int = 0) -> dict:
    key_list = jax.random.split(jax.random.key(seed), 7)
    tokens = normal_values(key_list[0], (TOKENS, WIDTH), 1.0, 6.0, ((0, 16), (1, 4)))
    weight = normal_values(key_list[1], (SECTIONS, WIDTH, WIDTH), WIDTH ** -0.5, 0.09375, ((0, 4), (1, 4), (2, 16)))
    out_grad = normal_values(key_list[2], (TOKENS, WIDTH), 1.0, 6.0, ((0, 16), (1, 4)))
    owner_index = plant(jax.random.randint(key_list[3], (SECTIONS,), 0, REPLICAS), jax.random.fold_in(key_list[3], 1), 0, REPLICAS - 1).astype(jnp.int32)
    input_factor = draw_input_factor(jax.random.fold_in(key_list[6], 71), 0)
    output_factor = draw_output_factor(jax.random.fold_in(key_list[6], 71), 0)
    return {"tokens": tokens, "weight": weight, "out_grad": out_grad, "owner_index": owner_index, "input_factor": input_factor, "output_factor": output_factor}


def activate(values):
    return jax.nn.gelu(values, approximate=True)

def gelu_back(hidden, cotangent):
    return jax.vjp(activate, hidden)[1](cotangent)[0]

def rounded(values):
    return lax.optimization_barrier(values.astype(jnp.bfloat16)).astype(jnp.float32)

def reference(tokens, weight, out_grad, owner_index, input_factor, output_factor):
    flowing = tokens
    inputs_kept = []
    hidden_kept = []
    for section_num in range(SECTIONS):
        split_in = flowing.astype(jnp.float32).reshape(TOKENS, WIDTH // BLOCK, BLOCK)
        split_weight = weight[section_num].astype(jnp.float32).reshape(WIDTH // BLOCK, BLOCK, WIDTH)
        partial_value = jnp.einsum('mnk,nkd->nmd', split_in, split_weight)
        hidden = lax.optimization_barrier(jnp.sum(rounded(partial_value), axis=0))
        inputs_kept.append(flowing)
        hidden_kept.append(hidden)
        flowing = (flowing.astype(jnp.float32) + activate(hidden)).astype(jnp.bfloat16)
    cotangent = out_grad
    grads_kept = [None] * SECTIONS
    for section_num in reversed(range(SECTIONS)):
        local_grad = gelu_back(hidden_kept[section_num], cotangent.astype(jnp.float32)).astype(jnp.bfloat16)
        grads_kept[section_num] = local_grad
        passed = jnp.dot(local_grad, weight[section_num].T, preferred_element_type=jnp.float32)
        cotangent = (cotangent.astype(jnp.float32) + passed).astype(jnp.bfloat16)
    results = []
    for section_num in range(SECTIONS):
        input_blocks = inputs_kept[section_num].reshape(REPLICAS, TOK_DEV, WIDTH)
        grad_blocks = grads_kept[section_num].reshape(REPLICAS, TOK_DEV, WIDTH)

        def accumulate(total, pair):
            term = jnp.dot(pair[0].T, pair[1], preferred_element_type=jnp.float32)
            return (total + rounded(term), None)
        summed, unused = lax.scan(accumulate, jnp.zeros((WIDTH, WIDTH), jnp.float32), (input_blocks, grad_blocks))
        scaled = summed / TOKENS
        factor = input_factor[section_num, owner_index[section_num]].reshape(WIDTH // BLOCK, BLOCK, BLOCK)
        left_applied = jnp.einsum('nij,njc->nic', factor, scaled.reshape(WIDTH // BLOCK, BLOCK, WIDTH), precision=lax.Precision.HIGHEST).reshape(WIDTH, WIDTH)
        right_factor = output_factor[section_num].reshape(WIDTH // OUT_BLOCK, OUT_BLOCK, OUT_BLOCK)
        preconditioned = jnp.einsum('rbi,bij->rbj', left_applied.reshape(WIDTH, WIDTH // OUT_BLOCK, OUT_BLOCK), right_factor, precision=lax.Precision.HIGHEST).reshape(WIDTH, WIDTH)
        results.append(preconditioned)
    return jnp.stack(results)
```

```python
import jax
import jax.numpy as jnp
from jax import lax
from jax.sharding import PartitionSpec as P

AXES = ("section", "dp", "tensor")
SECTIONS, HALVES, ROWS, CORES, COLUMNS = 4, 2, 4, 2, 4
PLANES = HALVES * SECTIONS
F32, BF16 = jnp.float32, jnp.bfloat16


def number(plane, y, core, x):
    half, section = plane // SECTIONS, plane % SECTIONS
    return (section * HALVES * ROWS * CORES + (half * ROWS + y) * CORES + core) * COLUMNS + x


def move(block, to):
    route = []
    for plane in range(PLANES):
        for y in range(ROWS):
            for core in range(CORES):
                for x in range(COLUMNS):
                    there = to(plane, y, core, x)
                    if there is not None:
                        route.append((number(plane, y, core, x), number(*there)))
    return lax.ppermute(block, AXES, route)


def push_z(block, by):
    return move(block, lambda z, y, c, x: ((z + by) % PLANES, y, c, x))


def push_y(block, by):
    return move(block, lambda z, y, c, x: (z, (y + by) % ROWS, c, x))


def push_x(block, by):
    return move(block, lambda z, y, c, x: (z, y, c, (x + by) % COLUMNS))


def flip_core(block):
    return move(block, lambda z, y, c, x: (z, y, 1 - c, x))


def rolled(blocks, start):
    twice = jnp.concatenate([blocks, blocks])
    return lax.dynamic_slice_in_dim(twice, start, blocks.shape[0], 0)


def by_chip(blocks):
    return jnp.stack([blocks[0], blocks[2], blocks[1], blocks[3]])


def activate(values):
    return jax.nn.gelu(values, approximate=True)


def gelu_back(hidden, cotangent):
    return jax.vjp(activate, hidden)[1](cotangent)[0]


def product(left, right, left_dim=1, right_dim=0):
    return lax.dot_general(
        left, right, (((left_dim,), (right_dim,)), ((), ())), preferred_element_type=F32
    )


def gather_weight(weight, place):
    plane, y, core, x = place
    rows, cols = weight.shape
    swap = lambda z, y, c, x: (z, 2 * c + y % 2, y // 2, x) if y // 2 != c else None
    weight = jnp.where(y // 2 == core, weight, move(weight, swap))
    weight = rolled(by_chip(weight.reshape(ROWS, rows // ROWS, cols)), y)
    streams = [weight[: ROWS // 2], weight[ROWS // 2 :]]
    held = jnp.zeros((PLANES, 2) + streams[0].shape, weight.dtype)

    def put(held, block, stream, distance):
        at = ((plane + distance) % PLANES, stream, 0, 0, 0)
        return lax.dynamic_update_slice(held, block[None, None], at)

    for stream in (0, 1):
        held = put(held, streams[stream], stream, 0)
    up, down = list(streams), list(streams)
    for step in range(1, PLANES // 2 + 1):
        for stream in (0, 1):
            if step < PLANES // 2 or stream == 0:
                up[stream] = push_z(up[stream], 1)
                held = put(held, up[stream], stream, -step)
            if step < PLANES // 2 or stream == 1:
                down[stream] = push_z(down[stream], -1)
                held = put(held, down[stream], stream, step)
    return held.reshape(HALVES, SECTIONS, rows, cols)


def section_weight(held, section, place):
    plane, y, core, x = place
    mine = held[:, section]
    other = flip_core(mine)
    blocks = []
    for k in range(COLUMNS):
        feature = (x + k) % COLUMNS
        own = lax.dynamic_index_in_dim(mine, feature // 2, 0, keepdims=False)
        got = lax.dynamic_index_in_dim(other, feature // 2, 0, keepdims=False)
        blocks.append(jnp.where(feature % 2 == core, own, got))
    return blocks


def fetch_factor(factor, owner, place):
    plane, y, core, x = place
    rank = (plane // SECTIONS * ROWS + y) * CORES + core
    value = jnp.where(rank == owner, factor.astype(BF16).T, jnp.zeros(factor.shape, BF16))
    steps = (
        (core, flip_core),
        (y % 2, lambda v: move(v, lambda z, y, c, x: (z, y ^ 1, c, x))),
        (y // 2, lambda v: move(v, lambda z, y, c, x: (z, y ^ 2, c, x))),
    )
    for bit, swap in steps:
        length = value.shape[0] // 2
        kept = lax.dynamic_slice_in_dim(value, bit * length, length, 0)
        given = lax.dynamic_slice_in_dim(value, (1 - bit) * length, length, 0)
        value = kept + swap(given)
    value = value + push_z(value, PLANES // 2)
    for bit, swap in steps[::-1]:
        got = swap(value)
        value = jnp.concatenate(
            [jnp.where(bit == 0, value, got), jnp.where(bit == 0, got, value)]
        )
    size = value.shape[0]
    blocks = rolled(by_chip(value.reshape(ROWS, size // ROWS, size)), y)
    return blocks.reshape(size, size)


def spread_right(factor, place):
    plane, y, core, x = place
    rows = factor.shape[0]
    value = factor.astype(BF16)
    kept = lax.dynamic_slice_in_dim(value, (y % 2) * 2 * rows, 2 * rows, 1)
    given = lax.dynamic_slice_in_dim(value, (1 - y % 2) * 2 * rows, 2 * rows, 1)
    got = move(given, lambda z, y, c, x: (z, y ^ 1, c, x))
    low = y % 2 == 0
    pair = jnp.stack([jnp.where(low, kept, got), jnp.where(low, got, kept)])
    other = flip_core(pair)
    first = core == 0
    blocks = jnp.concatenate([jnp.where(first, pair, other), jnp.where(first, other, pair)])
    return rolled(blocks, y).reshape(ROWS * rows, 2 * rows)


def body(tokens, weight, out_grad, owner_index, input_factor, output_factor):
    section, rank, x = (lax.axis_index(name) for name in AXES)
    half, y, core = rank // (ROWS * CORES), rank // CORES % ROWS, rank % CORES
    plane = half * SECTIONS + section
    place = (plane, y, core, x)
    width = weight.shape[2]
    share = tokens.shape[0] // SECTIONS
    total_tokens = tokens.shape[0] * HALVES * ROWS * CORES

    token_share = lax.dynamic_slice_in_dim(tokens, section * share, share, 0)
    grad_share = lax.dynamic_slice_in_dim(out_grad, section * share, share, 0)
    pieces = [token_share] + [push_y(token_share, -k) for k in range(1, ROWS)]
    flowing = rolled(jnp.stack(pieces), (ROWS - y) % ROWS)
    flowing = flowing.reshape(ROWS * share, ROWS, width).transpose(1, 0, 2)
    flowing = rolled(by_chip(flowing), y)
    flowing = [flowing[k] for k in range(ROWS)]

    grad_blocks = rolled(by_chip(grad_share.reshape(share, ROWS, width).transpose(1, 0, 2)), y)
    pieces = [grad_blocks[0]] + [push_y(grad_blocks[ROWS - k], -k) for k in range(1, ROWS)]
    cotangent = rolled(jnp.stack(pieces), (ROWS - y) % ROWS).reshape(ROWS * share, width)

    held = gather_weight(weight[0], place)
    weights = [section_weight(held, s, place) for s in range(SECTIONS)]

    inputs, hiddens = [], []
    for s in range(SECTIONS):
        full = jnp.concatenate(flowing, axis=1)
        inputs.append(full)
        parts = [product(full, weights[s][k]) for k in range(COLUMNS)]
        hidden = parts[0]
        for k in range(1, COLUMNS):
            hidden = hidden + push_x(parts[k].astype(BF16), k).astype(F32)
        hiddens.append(hidden)
        if s + 1 < SECTIONS:
            grown = (flowing[0].astype(F32) + activate(hidden)).astype(BF16)
            flowing = [grown] + [push_y(grown, -k) for k in range(1, ROWS)]

    grads = [None] * SECTIONS
    for s in reversed(range(SECTIONS)):
        local_grad = gelu_back(hiddens[s], cotangent.astype(F32)).astype(BF16)
        full = [local_grad] + [push_x(local_grad, -k) for k in range(1, COLUMNS)]
        grads[s] = jnp.stack(full)
        if s > 0:
            passed = sum(product(full[k], weights[s][k], 1, 1) for k in range(COLUMNS))
            new = cotangent.astype(F32) + passed[:, :width]
            for k in range(1, ROWS):
                sent = passed[:, k * width : (k + 1) * width].astype(BF16)
                new = new + push_y(sent, k).astype(F32)
            cotangent = new.astype(BF16)

    factor = fetch_factor(input_factor[0, 0], owner_index[0], place)
    right = spread_right(output_factor[0], place)

    inputs = jnp.stack(inputs)
    pieces = []
    for distance in range(PLANES):
        piece = lax.dynamic_index_in_dim(inputs, (section + distance) % SECTIONS, 0, False)
        pieces.append(push_z(piece, distance) if distance else piece)
    turned = product(jnp.concatenate(pieces), factor).astype(BF16)

    grads = jnp.stack(grads)
    pieces = []
    for distance in range(PLANES):
        aim = (plane + distance) % PLANES
        both = []
        for b in range(2):
            k = (2 * (aim // SECTIONS) + b - x) % COLUMNS
            at = (aim % SECTIONS, k, 0, 0)
            both.append(lax.dynamic_slice(grads, at, (1, 1) + grads.shape[2:])[0, 0])
        piece = jnp.concatenate(both, axis=1)
        pieces.append(push_z(piece, distance) if distance else piece)
    left = product(turned, jnp.concatenate(pieces), 0, 0) / total_tokens

    kept = lax.dynamic_slice_in_dim(left, core * width, width, 1)
    given = lax.dynamic_slice_in_dim(left, (1 - core) * width, width, 1)
    left = (kept + flip_core(given.astype(BF16)).astype(F32)).astype(BF16)

    def to_user(by):
        def to(z, y, c, x):
            there = (y + by) % ROWS
            return (z, there, c, x) if there // 2 == c else None

        return to

    pieces = [left] + [move(left, to_user(-k)) for k in range(1, ROWS)]
    both = product(jnp.concatenate(pieces, axis=1), right)
    kept = lax.dynamic_slice_in_dim(both, core * width, width, 1)
    given = lax.dynamic_slice_in_dim(both, (1 - core) * width, width, 1).astype(BF16)
    got = move(given, lambda z, y, c, x: (z, y, 1 - c, x) if y // 2 == c else None)
    result = jnp.where(y // 2 == core, kept, got.astype(F32))
    return result[None]


def solution(mesh):
    placed = (
        P("dp", "tensor"),
        P("section", "tensor", "dp"),
        P("dp", "tensor"),
        P("section"),
        P("section", "dp", "tensor", None),
        P("section", "dp", None),
    )
    return jax.shard_map(
        body, mesh=mesh, in_specs=placed, out_specs=P("section", "tensor", "dp"), check_vma=False
    )
```

```python
import jax
import jax.numpy as jnp
from jax import lax
from jax.sharding import Mesh, PartitionSpec as P

AXES = ("section", "half", "high", "low", "core", "tensor")
SIZES = (4, 2, 2, 2, 2, 4)
Z, Y, X = ("half", "section"), ("high", "low"), "tensor"
SECTIONS, PLANES, ROWS, COLUMNS = 4, 8, 4, 4
F32, BF16 = jnp.float32, jnp.bfloat16


def number(plane, y, core, x):
    half, section = plane // SECTIONS, plane % SECTIONS
    return ((section * 2 + half) * ROWS + y) * 8 + core * COLUMNS + x


def move(block, to):
    route = []
    for plane in range(PLANES):
        for y in range(ROWS):
            for core in range(2):
                for x in range(COLUMNS):
                    there = to(plane, y, core, x)
                    if there is not None:
                        route.append((number(plane, y, core, x), number(*there)))
    return lax.ppermute(block, AXES, route)


def push_z(block, by):
    return move(block, lambda z, y, c, x: ((z + by) % PLANES, y, c, x))


def flip_core(block):
    return move(block, lambda z, y, c, x: (z, y, 1 - c, x))


def trade(blocks, axis):
    return lax.all_to_all(blocks, axis, 0, 0)


def spread(block, axis, count):
    return trade(jnp.broadcast_to(block[None], (count,) + block.shape), axis)


def crossed(blocks):
    return [blocks[0], blocks[2], blocks[1], blocks[3]]


def tie(*values):
    return lax.optimization_barrier(values)


def activate(values):
    return jax.nn.gelu(values, approximate=True)


def gelu_back(hidden, cotangent):
    return jax.vjp(activate, hidden)[1](cotangent)[0]


def product(left, right, left_dim=1, right_dim=0):
    return lax.dot_general(
        left, right, (((left_dim,), (right_dim,)), ((), ())), preferred_element_type=F32
    )


def gather_weight(weight, plane, high, core, beside):
    stays = lambda y, c: y // 2 == c
    keep = high == core
    swap = lambda z, y, c, x: None if stays(y, c) else (z, 2 * c + y % 2, y // 2, x)

    def push(block, by, stay):
        def to(z, y, c, x):
            return ((z + by) % PLANES, y, c, x) if stays(y, c) == stay else None

        return move(block, to)

    swapped = move(weight, swap)
    start = {True: weight, False: swapped}
    held = jnp.zeros((PLANES,) + weight.shape, weight.dtype)

    def put(held, blocks, distance):
        block = jnp.where(keep, blocks[True], blocks[False])
        at = ((plane + distance) % PLANES, 0, 0)
        return lax.dynamic_update_slice(held, block[None], at)

    held = put(held, start, 0)
    up, down = dict(start), dict(start)
    for step in range(1, PLANES // 2):
        for stay in (True, False):
            up[stay] = push(up[stay], 1, stay)
            down[stay] = push(down[stay], -1, stay)
        if step == 2:
            up[True], *beside = tie(up[True], *beside)
        held = put(held, up, -step)
        held = put(held, down, step)
    last = {True: push(up[True], 1, True), False: push(down[False], -1, False)}
    held = put(held, last, PLANES // 2)
    return held.reshape((2, SECTIONS) + weight.shape), beside


def section_weight(held, section, core):
    mine = held[:, section]
    other = flip_core(mine)
    blocks = []
    for feature in range(COLUMNS):
        half, which = feature // 2, feature % 2
        blocks.append(jnp.where(core == which, mine[half], other[half]))
    return blocks


def halve_factor(factor, owner, rank, core):
    value = jnp.where(rank == owner, factor.astype(BF16), jnp.zeros(factor.shape, BF16))
    length = value.shape[0] // 2
    kept = lax.dynamic_slice_in_dim(value, core * length, length, 0)
    given = lax.dynamic_slice_in_dim(value, (1 - core) * length, length, 0)
    return kept + flip_core(given)


def total(blocks):
    return blocks[0] + blocks[1] + blocks[2] + blocks[3]


def join_factor(value, core):
    other = flip_core(value)
    first = core == 0
    return jnp.concatenate([jnp.where(first, value, other), jnp.where(first, other, value)])


def body(tokens, weight, out_grad, owner_index, input_factor, output_factor):
    section, half, high, low, core, x = (lax.axis_index(name) for name in AXES)
    y = high * 2 + low
    plane = half * SECTIONS + section
    quarter = low * 2 + high
    rank = (half * ROWS + y) * 2 + core
    width = weight.shape[2]
    share = tokens.shape[0] // SECTIONS
    tok = ROWS * share
    total_tokens = tokens.shape[0] * 16

    factor = halve_factor(input_factor[0, 0], owner_index[0], rank, core)
    token_share = lax.dynamic_slice_in_dim(tokens, section * share, share, 0)
    grad_share = lax.dynamic_slice_in_dim(out_grad, section * share, share, 0)
    held, (factor,) = gather_weight(weight[0], plane, high, core, (factor,))
    both = spread(jnp.stack([token_share, grad_share]), Y, ROWS)
    full = both[:, 0].reshape(tok, -1)
    flowing = lax.dynamic_slice_in_dim(full, quarter * width, width, 1)
    cotangent = lax.dynamic_slice_in_dim(both[:, 1].reshape(tok, -1), quarter * width, width, 1)

    factor = total(trade(factor.reshape(ROWS, -1, factor.shape[1]), Y))
    right = output_factor[0].astype(BF16)
    right = jnp.stack([right[:, : 2 * width], right[:, 2 * width :]])
    right = trade(jnp.repeat(right, 2, axis=0), ("low", "core")).reshape(ROWS * width, 2 * width)
    held, factor, right, full, cotangent = tie(held, factor, right, full, cotangent)
    weights = [section_weight(held, s, core) for s in range(SECTIONS)]

    inputs, hiddens, pieces = [], [], []

    factor = factor + push_z(factor, PLANES // 2)
    for s in range(SECTIONS):
        inputs.append(full)
        parts = jnp.stack([product(full, w).astype(BF16) for w in weights[s]])
        hidden = jnp.sum(trade(parts, X).astype(F32), axis=0)
        if s == 2:
            hidden, factor = tie(hidden, factor)
        if s == 3:
            factor = join_factor(factor, core)
            hidden, factor = tie(hidden, factor)
        hiddens.append(hidden)
        if s + 1 < SECTIONS:
            flowing = (flowing.astype(F32) + activate(hidden)).astype(BF16)
            full = jnp.concatenate(crossed(spread(flowing, Y, ROWS)), axis=1)
        if s == 0:
            full, factor = tie(full, factor)
            factor = spread(factor, Y, ROWS).reshape(-1, factor.shape[1])

    def quarter_of_inputs(at):
        sent = jnp.stack([v[:, at * width : (at + 1) * width] for v in inputs])
        return trade(jnp.concatenate([sent, sent]), Z)

    grads = [None] * SECTIONS
    for s in reversed(range(SECTIONS)):
        got = quarter_of_inputs(SECTIONS - 1 - s)
        local_grad = gelu_back(hiddens[s], cotangent.astype(F32)).astype(BF16)
        grad = spread(local_grad, X, COLUMNS)
        grads[s], got = tie(grad, got)
        inputs = list(tie(*inputs, grads[s]))[:SECTIONS]
        pieces.append(got.reshape(PLANES * tok, width))
        if s > 0:
            passed = sum(product(grads[s][k], weights[s][k], 1, 1) for k in range(COLUMNS))
            parts = jnp.stack(crossed(jnp.split(passed, ROWS, axis=1))).astype(BF16)
            new = cotangent.astype(F32) + jnp.sum(trade(parts, Y).astype(F32), axis=0)
            cotangent = new.astype(BF16)
    turned = product(jnp.concatenate(pieces, axis=1), factor, 1, 1).astype(BF16)

    sent = [jnp.concatenate([g[2 * h], g[2 * h + 1]], axis=1) for h in range(2) for g in grads]
    got = trade(jnp.stack(sent), Z).reshape(PLANES * tok, 2 * width)
    left = product(turned, got, 0, 0) / total_tokens

    kept = lax.dynamic_slice_in_dim(left, core * width, width, 1)
    given = lax.dynamic_slice_in_dim(left, (1 - core) * width, width, 1)
    left = (kept + flip_core(given.astype(BF16)).astype(F32)).astype(BF16)

    def to_user(by):
        def to(z, y, c, x):
            there = (y + by) % ROWS
            return (z, there, c, x) if there // 2 == c else None

        return to

    pieces = jnp.stack([left] + [move(left, to_user(-k)) for k in range(1, ROWS)])
    pieces = jnp.concatenate([pieces, pieces])
    pieces = lax.dynamic_slice_in_dim(pieces, (ROWS - y) % ROWS, ROWS, 0)
    both = product(jnp.concatenate(crossed(pieces), axis=1), right)
    kept = lax.dynamic_slice_in_dim(both, core * width, width, 1)
    given = lax.dynamic_slice_in_dim(both, (1 - core) * width, width, 1).astype(BF16)
    got = move(given, lambda z, y, c, x: (z, y, 1 - c, x) if y // 2 == c else None)
    result = jnp.where(high == core, kept, got.astype(F32))
    return result[None]


def solution(mesh):
    dp = ("half", "high", "low", "core")
    placed = (
        P(dp, "tensor"),
        P("section", "tensor", dp),
        P(dp, "tensor"),
        P("section"),
        P("section", dp, "tensor", None),
        P("section", dp, None),
    )
    fine = Mesh(mesh.devices.reshape(SIZES), AXES)
    return jax.shard_map(
        body, mesh=fine, in_specs=placed, out_specs=P("section", "tensor", dp), check_vma=False
    )
```

```python
import jax
import jax.numpy as jnp
from jax import lax
from jax.sharding import PartitionSpec as P

AXES = ("section", "dp", "tensor")
SECTIONS, HALVES, ROWS, CORES, COLUMNS = 4, 2, 4, 2, 4
PLANES = HALVES * SECTIONS
F32, BF16 = jnp.float32, jnp.bfloat16


def number(plane, y, core, x):
    half, section = plane // SECTIONS, plane % SECTIONS
    return (section * HALVES * ROWS * CORES + (half * ROWS + y) * CORES + core) * COLUMNS + x


def move(block, to):
    route = []
    for plane in range(PLANES):
        for y in range(ROWS):
            for core in range(CORES):
                for x in range(COLUMNS):
                    there = to(plane, y, core, x)
                    if there is not None:
                        route.append((number(plane, y, core, x), number(*there)))
    return lax.ppermute(block, AXES, route)


def push_z(block, by):
    return move(block, lambda z, y, c, x: ((z + by) % PLANES, y, c, x))


def push_y(block, by):
    return move(block, lambda z, y, c, x: (z, (y + by) % ROWS, c, x))


def push_x(block, by):
    return move(block, lambda z, y, c, x: (z, y, c, (x + by) % COLUMNS))


def flip_core(block):
    return move(block, lambda z, y, c, x: (z, y, 1 - c, x))


def rolled(blocks, start):
    twice = jnp.concatenate([blocks, blocks])
    return lax.dynamic_slice_in_dim(twice, start, blocks.shape[0], 0)


def natural(pieces, y):
    blocks = rolled(jnp.stack(pieces), (ROWS - y) % ROWS)
    return jnp.concatenate([blocks[0], blocks[2], blocks[1], blocks[3]], axis=1)


def quarter(values, chip):
    size = values.shape[1] // ROWS
    return lax.dynamic_slice_in_dim(values, (chip % 2 * 2 + chip // 2) * size, size, 1)


def tie(*values):
    return lax.optimization_barrier(values)


def activate(values):
    return jax.nn.gelu(values, approximate=True)


def gelu_back(hidden, cotangent):
    return jax.vjp(activate, hidden)[1](cotangent)[0]


def product(left, right, left_dim=1, right_dim=0):
    return lax.dot_general(
        left, right, (((left_dim,), (right_dim,)), ((), ())), preferred_element_type=F32
    )


def swap_weight(weight, place):
    plane, y, core, x = place
    swap = lambda z, y, c, x: (z, 2 * c + y % 2, y // 2, x) if y // 2 != c else None
    streams = jnp.split(weight, 2)
    return [jnp.where(y // 2 == core, part, move(part, swap)) for part in streams]


def gather_weight(streams, place):
    plane, y, core, x = place
    rows, cols = streams[0].shape
    held = jnp.zeros((PLANES, 2, rows, cols), streams[0].dtype)

    def put(held, block, stream, distance):
        at = ((plane + distance) % PLANES, stream, 0, 0)
        return lax.dynamic_update_slice(held, block[None, None], at)

    for stream in (0, 1):
        held = put(held, streams[stream], stream, 0)
    up, down = list(streams), list(streams)
    for step in range(1, PLANES // 2 + 1):
        for stream in (0, 1):
            if step < PLANES // 2 or stream == 0:
                up[stream] = push_z(up[stream], 1)
                held = put(held, up[stream], stream, -step)
            if step < PLANES // 2 or stream == 1:
                down[stream] = push_z(down[stream], -1)
                held = put(held, down[stream], stream, step)
    return held.reshape(HALVES, SECTIONS, 2 * rows, cols)


def section_weight(held, section, place):
    plane, y, core, x = place
    mine = held[:, section]
    other = flip_core(mine)
    blocks = []
    for k in range(COLUMNS):
        feature = (x + k) % COLUMNS
        own = lax.dynamic_index_in_dim(mine, feature // 2, 0, keepdims=False)
        got = lax.dynamic_index_in_dim(other, feature // 2, 0, keepdims=False)
        blocks.append(jnp.where(feature % 2 == core, own, got))
    return blocks


def flip_low(block):
    return move(block, lambda z, y, c, x: (z, y ^ 1, c, x))


def flip_high(block):
    return move(block, lambda z, y, c, x: (z, y ^ 2, c, x))


def halve_factor(factor, owner, place):
    plane, y, core, x = place
    rank = (plane // SECTIONS * ROWS + y) * CORES + core
    value = jnp.where(rank == owner, factor.astype(BF16), jnp.zeros(factor.shape, BF16))
    for bit, swap in ((core, flip_core), (y % 2, flip_low), (y // 2, flip_high)):
        length = value.shape[0] // 2
        kept = lax.dynamic_slice_in_dim(value, bit * length, length, 0)
        given = lax.dynamic_slice_in_dim(value, (1 - bit) * length, length, 0)
        value = kept + swap(given)
    return value


def double_factor(value, bit, swap):
    got = swap(value)
    return jnp.concatenate([jnp.where(bit == 0, value, got), jnp.where(bit == 0, got, value)])


def spread_right(factor, place):
    plane, y, core, x = place
    rows = factor.shape[0]
    value = factor.astype(BF16)
    kept = lax.dynamic_slice_in_dim(value, (y % 2) * 2 * rows, 2 * rows, 1)
    given = lax.dynamic_slice_in_dim(value, (1 - y % 2) * 2 * rows, 2 * rows, 1)
    got = flip_low(given)
    low = y % 2 == 0
    pair = jnp.stack([jnp.where(low, kept, got), jnp.where(low, got, kept)])
    other = flip_core(pair)
    first = core == 0
    blocks = jnp.concatenate([jnp.where(first, pair, other), jnp.where(first, other, pair)])
    return rolled(blocks, y).reshape(ROWS * rows, 2 * rows)


def reduce_gradient(block_for, beside):
    halves = lambda value: jnp.split(value, 2)
    far = halves(block_for(PLANES // 2))
    running = {(0, 1): far[0], (1, -1): far[1]}
    for step in range(1, PLANES // 2 + 1):
        for stream in (0, 1):
            for way in (1, -1):
                if (stream, way) in running:
                    running[stream, way] = push_z(running[stream, way], way)
        left = PLANES // 2 - step
        if left == 1:
            running[0, 1], *beside = tie(running[0, 1], *beside)
        if left > 0:
            for way in (1, -1):
                for stream, own in enumerate(halves(block_for(way * left))):
                    value = running.get((stream, way))
                    running[stream, way] = own if value is None else own + value
    own = halves(block_for(0))
    sums = []
    for stream in (0, 1):
        value = own[stream].astype(F32) + running[stream, 1].astype(F32)
        sums.append(value + running[stream, -1].astype(F32))
    return jnp.concatenate(sums), beside


def body(tokens, weight, out_grad, owner_index, input_factor, output_factor):
    section, rank, x = (lax.axis_index(name) for name in AXES)
    half, y, core = rank // (ROWS * CORES), rank // CORES % ROWS, rank % CORES
    plane = half * SECTIONS + section
    place = (plane, y, core, x)
    width = weight.shape[2]
    share = tokens.shape[0] // SECTIONS
    total_tokens = tokens.shape[0] * HALVES * ROWS * CORES

    streams = swap_weight(weight[0], place)
    streams[0], tokens, out_grad, input_factor = tie(streams[0], tokens, out_grad, input_factor)
    held = gather_weight(streams, place)

    token_share = lax.dynamic_slice_in_dim(tokens, section * share, share, 0)
    grad_share = lax.dynamic_slice_in_dim(out_grad, section * share, share, 0)
    pieces = []
    for k in range(ROWS):
        part = quarter(grad_share, (y + ROWS - k) % ROWS)
        both = jnp.concatenate([token_share, part], axis=1)
        pieces.append(push_y(both, -k) if k else both)
    both = rolled(jnp.stack(pieces), (ROWS - y) % ROWS).reshape(ROWS * share, -1)
    full, cotangent = both[:, : ROWS * width], both[:, ROWS * width :]
    flowing = quarter(full, y)

    factor = halve_factor(input_factor[0, 0], owner_index[0], place)
    held, factor, full, cotangent = tie(held, factor, full, cotangent)
    weights = [section_weight(held, s, place) for s in range(SECTIONS)]
    factor = factor + push_z(factor, PLANES // 2)

    inputs, hiddens = [], []
    for s in range(SECTIONS):
        inputs.append(full)
        parts = [product(full, weights[s][k]) for k in range(COLUMNS)]
        hidden = parts[0]
        for k in range(1, COLUMNS):
            hidden = hidden + push_x(parts[k].astype(BF16), k).astype(F32)
        hiddens.append(hidden)
        if s + 1 < SECTIONS:
            flowing = (flowing.astype(F32) + activate(hidden)).astype(BF16)
            full = natural([flowing] + [push_y(flowing, -k) for k in range(1, ROWS)], y)
        if s == 2:
            full, factor = tie(full, factor)

    inputs = jnp.stack(inputs)
    inputs = jnp.concatenate([inputs, flip_core(inputs)], axis=1)

    grads = [None] * SECTIONS
    for s in reversed(range(SECTIONS)):
        local_grad = gelu_back(hiddens[s], cotangent.astype(F32)).astype(BF16)
        grad = [local_grad] + [push_x(local_grad, -k) for k in range(1, COLUMNS)]
        grads[s] = rolled(jnp.stack(grad), (COLUMNS - x) % COLUMNS)
        if s > 0:
            passed = sum(product(grad[k], weights[s][k], 1, 1) for k in range(COLUMNS))
            new = cotangent.astype(F32) + quarter(passed, y)
            for k in range(1, ROWS):
                sent = quarter(passed, (y + k) % ROWS).astype(BF16)
                new = new + push_y(sent, k).astype(F32)
            cotangent = new.astype(BF16)
        if s == 1:
            cotangent, inputs = tie(cotangent, inputs)

    grads = jnp.stack(grads)
    grads = grads.reshape(SECTIONS, HALVES, CORES, *local_grad.shape)
    kept = lax.dynamic_index_in_dim(grads, core, 2, keepdims=False)
    given = lax.dynamic_index_in_dim(grads, 1 - core, 2, keepdims=False)
    grads = jnp.concatenate([kept, flip_core(given)], axis=2)

    def block_for(distance):
        aim = (plane + distance) % PLANES
        at, which = aim % SECTIONS, aim // SECTIONS
        chosen = lax.dynamic_index_in_dim(inputs, at, 0, keepdims=False)
        grad = lax.dynamic_slice(grads, (at, which, 0, 0), (1, 1) + grads.shape[2:])[0, 0]
        return product(chosen, grad, 0, 0).astype(BF16)

    for bit, swap in ((y // 2, flip_high), (y % 2, flip_low), (core, flip_core)):
        factor = double_factor(factor, bit, swap)
    right = spread_right(output_factor[0], place)
    gradient, (factor, right) = reduce_gradient(block_for, (factor, right))
    gradient = (gradient / total_tokens).astype(BF16)
    left = product(factor, gradient).astype(BF16)

    def to_user(by):
        def to(z, y, c, x):
            there = (y + by) % ROWS
            return (z, there, c, x) if there // 2 == c else None

        return to

    pieces = [left] + [move(left, to_user(-k)) for k in range(1, ROWS)]
    both = product(jnp.concatenate(pieces, axis=1), right)
    kept = lax.dynamic_slice_in_dim(both, core * width, width, 1)
    given = lax.dynamic_slice_in_dim(both, (1 - core) * width, width, 1).astype(BF16)
    got = move(given, lambda z, y, c, x: (z, y, 1 - c, x) if y // 2 == c else None)
    result = jnp.where(y // 2 == core, kept, got.astype(F32))
    return result[None]


def solution(mesh):
    placed = (
        P("dp", "tensor"),
        P("section", "tensor", "dp"),
        P("dp", "tensor"),
        P("section"),
        P("section", "dp", "tensor", None),
        P("section", "dp", None),
    )
    return jax.shard_map(
        body, mesh=mesh, in_specs=placed, out_specs=P("section", "tensor", "dp"), check_vma=False
    )
```

```python
import jax
import jax.numpy as jnp
from jax import lax
from jax.sharding import PartitionSpec as P

AXES = ("section", "dp", "tensor")
SECTIONS, HALVES, ROWS, CORES, COLUMNS = 4, 2, 4, 2, 4
PLANES = HALVES * SECTIONS
F32, BF16 = jnp.float32, jnp.bfloat16


def number(plane, y, core, x):
    half, section = plane // SECTIONS, plane % SECTIONS
    return (section * HALVES * ROWS * CORES + (half * ROWS + y) * CORES + core) * COLUMNS + x


def move(block, to):
    route = []
    for plane in range(PLANES):
        for y in range(ROWS):
            for core in range(CORES):
                for x in range(COLUMNS):
                    there = to(plane, y, core, x)
                    if there is not None:
                        route.append((number(plane, y, core, x), number(*there)))
    return lax.ppermute(block, AXES, route)


def push_z(block, by):
    return move(block, lambda z, y, c, x: ((z + by) % PLANES, y, c, x))


def push_y(block, by):
    return move(block, lambda z, y, c, x: (z, (y + by) % ROWS, c, x))


def push_x(block, by):
    return move(block, lambda z, y, c, x: (z, y, c, (x + by) % COLUMNS))


def flip_core(block):
    return move(block, lambda z, y, c, x: (z, y, 1 - c, x))


def rolled(blocks, start):
    twice = jnp.concatenate([blocks, blocks])
    return lax.dynamic_slice_in_dim(twice, start, blocks.shape[0], 0)


def natural(pieces, y):
    blocks = rolled(jnp.stack(pieces), (ROWS - y) % ROWS)
    return jnp.concatenate([blocks[0], blocks[2], blocks[1], blocks[3]], axis=1)


def quarter(values, chip):
    size = values.shape[1] // ROWS
    return lax.dynamic_slice_in_dim(values, (chip % 2 * 2 + chip // 2) * size, size, 1)


def tie(*values):
    return lax.optimization_barrier(values)


def activate(values):
    return jax.nn.gelu(values, approximate=True)


def gelu_back(hidden, cotangent):
    return jax.vjp(activate, hidden)[1](cotangent)[0]


def product(left, right, left_dim=1, right_dim=0):
    return lax.dot_general(
        left, right, (((left_dim,), (right_dim,)), ((), ())), preferred_element_type=F32
    )


def swap_weight(weight, place):
    plane, y, core, x = place
    swap = lambda z, y, c, x: (z, 2 * c + y % 2, y // 2, x) if y // 2 != c else None
    streams = jnp.split(weight, 2)
    return [jnp.where(y // 2 == core, part, move(part, swap)) for part in streams]


def gather_weight(streams, place, beside):
    plane, y, core, x = place
    rows, cols = streams[0].shape
    held = jnp.zeros((PLANES, 2, rows, cols), streams[0].dtype)

    def put(held, block, stream, distance):
        at = ((plane + distance) % PLANES, stream, 0, 0)
        return lax.dynamic_update_slice(held, block[None, None], at)

    for stream in (0, 1):
        held = put(held, streams[stream], stream, 0)
    up, down = list(streams), list(streams)
    value = None
    for step in range(1, PLANES // 2 + 1):
        if step > 1:
            down[1], value = tie(down[1], value)
        if step <= len(beside):
            value = beside[step - 1](value)
        for stream in (0, 1):
            if step < PLANES // 2 or stream == 0:
                up[stream] = push_z(up[stream], 1)
                held = put(held, up[stream], stream, -step)
            if step < PLANES // 2 or stream == 1:
                down[stream] = push_z(down[stream], -1)
                held = put(held, down[stream], stream, step)
    return held.reshape(HALVES, SECTIONS, 2 * rows, cols), value


def section_weight(held, section, place):
    plane, y, core, x = place
    mine = held[:, section]
    other = flip_core(mine)
    blocks = []
    for k in range(COLUMNS):
        feature = (x + k) % COLUMNS
        own = lax.dynamic_index_in_dim(mine, feature // 2, 0, keepdims=False)
        got = lax.dynamic_index_in_dim(other, feature // 2, 0, keepdims=False)
        blocks.append(jnp.where(feature % 2 == core, own, got))
    return blocks


def flip_low(block):
    return move(block, lambda z, y, c, x: (z, y ^ 1, c, x))


def flip_high(block):
    return move(block, lambda z, y, c, x: (z, y ^ 2, c, x))


def halve(value, bit, swap):
    length = value.shape[0] // 2
    kept = lax.dynamic_slice_in_dim(value, bit * length, length, 0)
    given = lax.dynamic_slice_in_dim(value, (1 - bit) * length, length, 0)
    return kept + swap(given)


def double_factor(value, bit, swap):
    got = swap(value)
    return jnp.concatenate([jnp.where(bit == 0, value, got), jnp.where(bit == 0, got, value)])


def spread_right(factor, place):
    plane, y, core, x = place
    rows = factor.shape[0]
    value = factor.astype(BF16)
    kept = lax.dynamic_slice_in_dim(value, (y % 2) * 2 * rows, 2 * rows, 1)
    given = lax.dynamic_slice_in_dim(value, (1 - y % 2) * 2 * rows, 2 * rows, 1)
    got = flip_low(given)
    low = y % 2 == 0
    pair = jnp.stack([jnp.where(low, kept, got), jnp.where(low, got, kept)])
    other = flip_core(pair)
    first = core == 0
    blocks = jnp.concatenate([jnp.where(first, pair, other), jnp.where(first, other, pair)])
    return rolled(blocks, y).reshape(ROWS * rows, 2 * rows)


def reduce_gradient(block_for, beside):
    halves = lambda value: jnp.split(value, 2)
    far = halves(block_for(PLANES // 2))
    running = {(0, 1): far[0], (1, -1): far[1]}
    for step in range(1, PLANES // 2 + 1):
        for stream in (0, 1):
            for way in (1, -1):
                if (stream, way) in running:
                    running[stream, way] = push_z(running[stream, way], way)
        left = PLANES // 2 - step
        if left == 1:
            running[0, 1], *beside = tie(running[0, 1], *beside)
        if left > 0:
            for way in (1, -1):
                for stream, own in enumerate(halves(block_for(way * left))):
                    value = running.get((stream, way))
                    running[stream, way] = own if value is None else own + value
    own = halves(block_for(0))
    sums = []
    for stream in (0, 1):
        value = own[stream].astype(F32) + running[stream, 1].astype(F32)
        sums.append(value + running[stream, -1].astype(F32))
    return jnp.concatenate(sums), beside


def body(tokens, weight, out_grad, owner_index, input_factor, output_factor):
    section, rank, x = (lax.axis_index(name) for name in AXES)
    half, y, core = rank // (ROWS * CORES), rank // CORES % ROWS, rank % CORES
    plane = half * SECTIONS + section
    place = (plane, y, core, x)
    width = weight.shape[2]
    share = tokens.shape[0] // SECTIONS
    total_tokens = tokens.shape[0] * HALVES * ROWS * CORES

    streams = swap_weight(weight[0], place)
    streams[0], input_factor = tie(streams[0], input_factor)

    def owned(unused):
        factor = input_factor[0, 0].astype(BF16)
        value = jnp.where(rank == owner_index[0], factor, jnp.zeros_like(factor))
        return halve(value, core, flip_core)

    steps = (
        owned,
        lambda value: halve(value, y % 2, flip_low),
        lambda value: halve(value, y // 2, flip_high),
    )
    held, factor = gather_weight(streams, place, steps)

    token_share = lax.dynamic_slice_in_dim(tokens, section * share, share, 0)
    grad_share = lax.dynamic_slice_in_dim(out_grad, section * share, share, 0)
    pieces = []
    for k in range(ROWS):
        part = quarter(grad_share, (y + ROWS - k) % ROWS)
        both = jnp.concatenate([token_share, part], axis=1)
        pieces.append(push_y(both, -k) if k else both)
    both = rolled(jnp.stack(pieces), (ROWS - y) % ROWS).reshape(ROWS * share, -1)
    full, cotangent = both[:, : ROWS * width], both[:, ROWS * width :]
    flowing = quarter(full, y)

    weights = [section_weight(held, s, place) for s in range(SECTIONS)]
    factor = factor + push_z(factor, PLANES // 2)

    inputs, hiddens = [], []
    for s in range(SECTIONS):
        inputs.append(full)
        parts = [product(full, weights[s][k]) for k in range(COLUMNS)]
        hidden = parts[0]
        for k in range(1, COLUMNS):
            hidden = hidden + push_x(parts[k].astype(BF16), k).astype(F32)
        hiddens.append(hidden)
        if s + 1 < SECTIONS:
            flowing = (flowing.astype(F32) + activate(hidden)).astype(BF16)
            full = natural([flowing] + [push_y(flowing, -k) for k in range(1, ROWS)], y)
        if s == 2:
            full, factor = tie(full, factor)

    inputs = jnp.stack(inputs)
    inputs = jnp.concatenate([inputs, flip_core(inputs)], axis=1)

    grads = [None] * SECTIONS
    for s in reversed(range(SECTIONS)):
        local_grad = gelu_back(hiddens[s], cotangent.astype(F32)).astype(BF16)
        grad = [local_grad] + [push_x(local_grad, -k) for k in range(1, COLUMNS)]
        grads[s] = rolled(jnp.stack(grad), (COLUMNS - x) % COLUMNS)
        if s > 0:
            passed = sum(product(grad[k], weights[s][k], 1, 1) for k in range(COLUMNS))
            new = cotangent.astype(F32) + quarter(passed, y)
            for k in range(1, ROWS):
                sent = quarter(passed, (y + k) % ROWS).astype(BF16)
                new = new + push_y(sent, k).astype(F32)
            cotangent = new.astype(BF16)
        if s == 1:
            cotangent, inputs = tie(cotangent, inputs)

    grads = jnp.stack(grads)
    grads = grads.reshape(SECTIONS, HALVES, CORES, *local_grad.shape)
    kept = lax.dynamic_index_in_dim(grads, core, 2, keepdims=False)
    given = lax.dynamic_index_in_dim(grads, 1 - core, 2, keepdims=False)
    grads = jnp.concatenate([kept, flip_core(given)], axis=2)

    def block_for(distance):
        aim = (plane + distance) % PLANES
        at, which = aim % SECTIONS, aim // SECTIONS
        chosen = lax.dynamic_index_in_dim(inputs, at, 0, keepdims=False)
        grad = lax.dynamic_slice(grads, (at, which, 0, 0), (1, 1) + grads.shape[2:])[0, 0]
        return product(chosen, grad, 0, 0).astype(BF16)

    for bit, swap in ((y // 2, flip_high), (y % 2, flip_low), (core, flip_core)):
        factor = double_factor(factor, bit, swap)
    right = spread_right(output_factor[0], place)
    gradient, (factor, right) = reduce_gradient(block_for, (factor, right))
    gradient = (gradient / total_tokens).astype(BF16)
    left = product(factor, gradient).astype(BF16)

    def to_user(by):
        def to(z, y, c, x):
            there = (y + by) % ROWS
            return (z, there, c, x) if there // 2 == c else None

        return to

    near, far = jnp.split(left, 2)

    def halfway(z, y, c, x):
        return (z, (y - 1) % ROWS, c, x) if (y - 2) % ROWS // 2 == c else None

    far = move(move(far, halfway), to_user(-1))
    pieces = [left, move(left, to_user(-1)), None, move(left, to_user(1))]
    pieces[2] = jnp.concatenate([move(near, to_user(2)), far])
    both = product(jnp.concatenate(pieces, axis=1), right)
    kept = lax.dynamic_slice_in_dim(both, core * width, width, 1)
    given = lax.dynamic_slice_in_dim(both, (1 - core) * width, width, 1).astype(BF16)
    got = move(given, lambda z, y, c, x: (z, y, 1 - c, x) if y // 2 == c else None)
    result = jnp.where(y // 2 == core, kept, got.astype(F32))
    return result[None]


def solution(mesh):
    placed = (
        P("dp", "tensor"),
        P("section", "tensor", "dp"),
        P("dp", "tensor"),
        P("section"),
        P("section", "dp", "tensor", None),
        P("section", "dp", None),
    )
    return jax.shard_map(
        body, mesh=mesh, in_specs=placed, out_specs=P("section", "tensor", "dp"), check_vma=False
    )
```

```python
import jax
import jax.numpy as jnp
from jax import lax
from jax.sharding import PartitionSpec as P

AXES = ("section", "dp", "tensor")
SECTIONS, HALVES, ROWS, CORES, COLUMNS = 4, 2, 4, 2, 4
PLANES = HALVES * SECTIONS
F32, BF16 = jnp.float32, jnp.bfloat16


def number(plane, y, core, x):
    half, section = plane // SECTIONS, plane % SECTIONS
    return (section * HALVES * ROWS * CORES + (half * ROWS + y) * CORES + core) * COLUMNS + x


def move(block, to):
    route = []
    for plane in range(PLANES):
        for y in range(ROWS):
            for core in range(CORES):
                for x in range(COLUMNS):
                    there = to(plane, y, core, x)
                    if there is not None:
                        route.append((number(plane, y, core, x), number(*there)))
    return lax.ppermute(block, AXES, route)


def push_z(block, by):
    return move(block, lambda z, y, c, x: ((z + by) % PLANES, y, c, x))


def flip_y(block, mask):
    return move(block, lambda z, y, c, x: (z, y ^ mask, c, x))


def push_x(block, by):
    return move(block, lambda z, y, c, x: (z, y, c, (x + by) % COLUMNS))


def flip_core(block):
    return move(block, lambda z, y, c, x: (z, y, 1 - c, x))


def rolled(blocks, start):
    twice = jnp.concatenate([blocks, blocks])
    return lax.dynamic_slice_in_dim(twice, start, blocks.shape[0], 0)


def natural(pieces, y, axis):
    blocks = []
    for chip in (0, 2, 1, 3):
        block = pieces[chip]
        for m in range(1, ROWS):
            block = jnp.where(y == m, pieces[chip ^ m], block)
        blocks.append(block)
    return jnp.concatenate(blocks, axis=axis)


def quarter(values, chip):
    size = values.shape[1] // ROWS
    return lax.dynamic_slice_in_dim(values, (chip % 2 * 2 + chip // 2) * size, size, 1)


def tie(*values):
    return lax.optimization_barrier(values)


def activate(values):
    return jax.nn.gelu(values, approximate=True)


def gelu_back(hidden, cotangent):
    return jax.vjp(activate, hidden)[1](cotangent)[0]


def product(left, right, left_dim=1, right_dim=0):
    return lax.dot_general(
        left, right, (((left_dim,), (right_dim,)), ((), ())), preferred_element_type=F32
    )


def stays(y, core):
    return y // 2 == core


def gather_weight(weight, swapped, place, beside):
    plane, y, core, x = place
    keep = stays(y, core)

    def push(block, by, stay):
        def to(z, y, c, x):
            return ((z + by) % PLANES, y, c, x) if stays(y, c) == stay else None

        return move(block, to)

    start = {True: weight, False: swapped}
    held = jnp.zeros((PLANES,) + weight.shape, weight.dtype)

    def put(held, blocks, distance):
        block = jnp.where(keep, blocks[True], blocks[False])
        at = ((plane + distance) % PLANES, 0, 0)
        return lax.dynamic_update_slice(held, block[None], at)

    held = put(held, start, 0)
    up, down = dict(start), dict(start)
    for step in range(1, PLANES // 2):
        if step == 3:
            down[False], *beside = tie(down[False], *beside)
        for stay in (True, False):
            up[stay] = push(up[stay], 1, stay)
            down[stay] = push(down[stay], -1, stay)
        held = put(held, up, -step)
        held = put(held, down, step)
    last = {True: push(up[True], 1, True), False: push(down[False], -1, False)}
    held = put(held, last, PLANES // 2)
    return held.reshape((HALVES, SECTIONS) + weight.shape), beside


def section_weight(held, section, place):
    plane, y, core, x = place
    mine = held[:, section]
    other = flip_core(mine)
    blocks = []
    for k in range(COLUMNS):
        feature = (x + k) % COLUMNS
        own = lax.dynamic_index_in_dim(mine, feature // 2, 0, keepdims=False)
        got = lax.dynamic_index_in_dim(other, feature // 2, 0, keepdims=False)
        blocks.append(jnp.where(feature % 2 == core, own, got))
    return blocks


def halve(value, bit, swap):
    length = value.shape[0] // 2
    kept = lax.dynamic_slice_in_dim(value, bit * length, length, 0)
    given = lax.dynamic_slice_in_dim(value, (1 - bit) * length, length, 0)
    return kept + swap(given)


def double_factor(value, bit, swap):
    got = swap(value)
    return jnp.concatenate([jnp.where(bit == 0, value, got), jnp.where(bit == 0, got, value)])


def spread_right(factor, place):
    plane, y, core, x = place
    rows = factor.shape[0]
    value = factor.astype(BF16)
    kept = lax.dynamic_slice_in_dim(value, (y % 2) * 2 * rows, 2 * rows, 1)
    given = lax.dynamic_slice_in_dim(value, (1 - y % 2) * 2 * rows, 2 * rows, 1)
    got = flip_y(given, 1)
    low = y % 2 == 0
    pair = jnp.stack([jnp.where(low, kept, got), jnp.where(low, got, kept)])
    other = flip_core(pair)
    first = core == 0
    blocks = jnp.concatenate([jnp.where(first, pair, other), jnp.where(first, other, pair)])
    return rolled(blocks, y).reshape(ROWS * rows, 2 * rows)


def reduce_gradient(block_for, beside):
    halves = lambda value: jnp.split(value, 2)
    far = halves(block_for(PLANES // 2))
    running = {(0, 1): far[0], (1, -1): far[1]}
    for step in range(1, PLANES // 2 + 1):
        for stream in (0, 1):
            for way in (1, -1):
                if (stream, way) in running:
                    running[stream, way] = push_z(running[stream, way], way)
        left = PLANES // 2 - step
        if left == 1:
            running[0, 1], *beside = tie(running[0, 1], *beside)
        if left > 0:
            for way in (1, -1):
                for stream, own in enumerate(halves(block_for(way * left))):
                    value = running.get((stream, way))
                    running[stream, way] = own if value is None else own + value
    own = halves(block_for(0))
    sums = []
    for stream in (0, 1):
        value = own[stream].astype(F32) + running[stream, 1].astype(F32)
        sums.append(value + running[stream, -1].astype(F32))
    return jnp.concatenate(sums), beside


def body(tokens, weight, out_grad, owner_index, input_factor, output_factor):
    section, rank, x = (lax.axis_index(name) for name in AXES)
    half, y, core = rank // (ROWS * CORES), rank // CORES % ROWS, rank % CORES
    plane = half * SECTIONS + section
    place = (plane, y, core, x)
    width = weight.shape[2]
    share = tokens.shape[0] // SECTIONS
    total_tokens = tokens.shape[0] * HALVES * ROWS * CORES

    low = lambda value: flip_y(value, 1)
    high = lambda value: flip_y(value, 2)

    swap = lambda z, y, c, x: None if stays(y, c) else (z, 2 * c + y % 2, y // 2, x)
    swapped = move(weight[0], swap)
    swapped, input_factor, tokens, out_grad = tie(swapped, input_factor, tokens, out_grad)

    token_share = lax.dynamic_slice_in_dim(tokens, section * share, share, 0)
    grad_share = lax.dynamic_slice_in_dim(out_grad, section * share, share, 0)
    pieces = []
    for mask in range(ROWS):
        part = quarter(grad_share, y ^ mask)
        both = jnp.concatenate([token_share, part], axis=1)
        pieces.append(flip_y(both, mask) if mask else both)
    both = natural(pieces, y, 0)
    full, cotangent = both[:, : ROWS * width], both[:, ROWS * width :]
    flowing = quarter(full, y)

    factor = input_factor[0, 0].astype(BF16)
    factor = jnp.where(rank == owner_index[0], factor, jnp.zeros_like(factor))
    factor = halve(factor, core, flip_core)
    beside = (full, flowing, cotangent, factor)
    held, (full, flowing, cotangent, factor) = gather_weight(weight[0], swapped, place, beside)
    weights = [section_weight(held, s, place) for s in range(SECTIONS)]

    inputs, hiddens = [], []
    for s in range(SECTIONS):
        inputs.append(full)
        parts = [product(full, weights[s][k]) for k in range(COLUMNS)]
        hidden = parts[0]
        for k in range(1, COLUMNS):
            hidden = hidden + push_x(parts[k].astype(BF16), k).astype(F32)
        hiddens.append(hidden)
        if s + 1 < SECTIONS:
            flowing = (flowing.astype(F32) + activate(hidden)).astype(BF16)
            pieces = [flowing] + [flip_y(flowing, mask) for mask in range(1, ROWS)]
            full = natural(pieces, y, 1)
        if s == 0:
            factor = halve(factor, y % 2, low)
        elif s == 1:
            factor = halve(factor, y // 2, high)
        elif s == 2:
            factor = factor + push_z(factor, PLANES // 2)
        if s < 2:
            full, factor = tie(full, factor)

    inputs = jnp.stack(inputs)
    inputs = jnp.concatenate([inputs, flip_core(inputs)], axis=1)

    grads = [None] * SECTIONS
    for s in reversed(range(SECTIONS)):
        local_grad = gelu_back(hiddens[s], cotangent.astype(F32)).astype(BF16)
        grad = [local_grad] + [push_x(local_grad, -k) for k in range(1, COLUMNS)]
        grads[s] = rolled(jnp.stack(grad), (COLUMNS - x) % COLUMNS)
        if s > 0:
            passed = sum(product(grad[k], weights[s][k], 1, 1) for k in range(COLUMNS))
            new = cotangent.astype(F32) + quarter(passed, y)
            for mask in range(1, ROWS):
                sent = quarter(passed, y ^ mask).astype(BF16)
                new = new + flip_y(sent, mask).astype(F32)
            cotangent = new.astype(BF16)
            bit, swap = ((core, flip_core), (y % 2, low), (y // 2, high))[s - 1]
            factor = double_factor(factor, bit, swap)
            if s > 1:
                cotangent, factor = tie(cotangent, factor)
        if s == 1:
            cotangent, inputs = tie(cotangent, inputs)

    grads = jnp.stack(grads)
    grads = grads.reshape(SECTIONS, HALVES, CORES, *local_grad.shape)
    kept = lax.dynamic_index_in_dim(grads, core, 2, keepdims=False)
    given = lax.dynamic_index_in_dim(grads, 1 - core, 2, keepdims=False)
    grads = jnp.concatenate([kept, flip_core(given)], axis=2)

    def block_for(distance):
        aim = (plane + distance) % PLANES
        at, which = aim % SECTIONS, aim // SECTIONS
        chosen = lax.dynamic_index_in_dim(inputs, at, 0, keepdims=False)
        grad = lax.dynamic_slice(grads, (at, which, 0, 0), (1, 1) + grads.shape[2:])[0, 0]
        return product(chosen, grad, 0, 0).astype(BF16)

    right = spread_right(output_factor[0], place)
    gradient, (factor, right) = reduce_gradient(block_for, (factor, right))
    gradient = (gradient / total_tokens).astype(BF16)
    left = product(factor, gradient).astype(BF16)

    def to_user(by):
        def to(z, y, c, x):
            there = (y + by) % ROWS
            return (z, there, c, x) if there // 2 == c else None

        return to

    near, far = jnp.split(left, 2)

    def halfway(z, y, c, x):
        return (z, (y - 1) % ROWS, c, x) if (y - 2) % ROWS // 2 == c else None

    far = move(move(far, halfway), to_user(-1))
    pieces = [left, move(left, to_user(-1)), None, move(left, to_user(1))]
    pieces[2] = jnp.concatenate([move(near, to_user(2)), far])
    both = product(jnp.concatenate(pieces, axis=1), right)
    kept = lax.dynamic_slice_in_dim(both, core * width, width, 1)
    given = lax.dynamic_slice_in_dim(both, (1 - core) * width, width, 1).astype(BF16)
    got = move(given, lambda z, y, c, x: (z, y, 1 - c, x) if y // 2 == c else None)
    result = jnp.where(y // 2 == core, kept, got.astype(F32))
    return result[None]


def solution(mesh):
    placed = (
        P("dp", "tensor"),
        P("section", "tensor", "dp"),
        P("dp", "tensor"),
        P("section"),
        P("section", "dp", "tensor", None),
        P("section", "dp", None),
    )
    return jax.shard_map(
        body, mesh=mesh, in_specs=placed, out_specs=P("section", "tensor", "dp"), check_vma=False
    )
```

```python
import jax
import jax.numpy as jnp
from jax import lax
from jax.sharding import PartitionSpec as P

AXES = ("section", "dp", "tensor")
SECTIONS, HALVES, ROWS, CORES, COLUMNS = 4, 2, 4, 2, 4
PLANES = HALVES * SECTIONS
F32, BF16 = jnp.float32, jnp.bfloat16


def number(plane, y, core, x):
    half, section = plane // SECTIONS, plane % SECTIONS
    return (section * HALVES * ROWS * CORES + (half * ROWS + y) * CORES + core) * COLUMNS + x


def move(block, to):
    route = []
    for plane in range(PLANES):
        for y in range(ROWS):
            for core in range(CORES):
                for x in range(COLUMNS):
                    there = to(plane, y, core, x)
                    if there is not None:
                        route.append((number(plane, y, core, x), number(*there)))
    return lax.ppermute(block, AXES, route)


def push_z(block, by):
    return move(block, lambda z, y, c, x: ((z + by) % PLANES, y, c, x))


def flip_y(block, mask):
    return move(block, lambda z, y, c, x: (z, y ^ mask, c, x))


def push_x(block, by):
    return move(block, lambda z, y, c, x: (z, y, c, (x + by) % COLUMNS))


def flip_core(block):
    return move(block, lambda z, y, c, x: (z, y, 1 - c, x))


def rolled(blocks, start):
    twice = jnp.concatenate([blocks, blocks])
    return lax.dynamic_slice_in_dim(twice, start, blocks.shape[0], 0)


def natural(pieces, y, axis):
    blocks = []
    for chip in (0, 2, 1, 3):
        block = pieces[chip]
        for m in range(1, ROWS):
            block = jnp.where(y == m, pieces[chip ^ m], block)
        blocks.append(block)
    return jnp.concatenate(blocks, axis=axis)


def quarter(values, chip):
    size = values.shape[1] // ROWS
    return lax.dynamic_slice_in_dim(values, (chip % 2 * 2 + chip // 2) * size, size, 1)


def tie(*values):
    return lax.optimization_barrier(values)


def activate(values):
    return jax.nn.gelu(values, approximate=True)


def gelu_back(hidden, cotangent):
    return jax.vjp(activate, hidden)[1](cotangent)[0]


def product(left, right, left_dim=1, right_dim=0):
    return lax.dot_general(
        left, right, (((left_dim,), (right_dim,)), ((), ())), preferred_element_type=F32
    )


def swap_weight(weight, place):
    plane, y, core, x = place
    swap = lambda z, y, c, x: (z, 2 * c + y % 2, y // 2, x) if y // 2 != c else None
    streams = jnp.split(weight, 2)
    return [jnp.where(y // 2 == core, part, move(part, swap)) for part in streams]


def gather_weight(streams, place, beside):
    plane, y, core, x = place
    rows, cols = streams[0].shape
    held = jnp.zeros((PLANES, 2, rows, cols), streams[0].dtype)

    def put(held, block, stream, distance):
        at = ((plane + distance) % PLANES, stream, 0, 0)
        return lax.dynamic_update_slice(held, block[None, None], at)

    for stream in (0, 1):
        held = put(held, streams[stream], stream, 0)
    up, down = list(streams), list(streams)
    for step in range(1, PLANES // 2 + 1):
        if step == 3:
            down[1], *beside = tie(down[1], *beside)
        for stream in (0, 1):
            if step < PLANES // 2 or stream == 0:
                up[stream] = push_z(up[stream], 1)
                held = put(held, up[stream], stream, -step)
            if step < PLANES // 2 or stream == 1:
                down[stream] = push_z(down[stream], -1)
                held = put(held, down[stream], stream, step)
    return held.reshape(HALVES, SECTIONS, 2 * rows, cols), beside


def section_weight(held, section, place):
    plane, y, core, x = place
    mine = held[:, section]
    other = flip_core(mine)
    blocks = []
    for k in range(COLUMNS):
        feature = (x + k) % COLUMNS
        own = lax.dynamic_index_in_dim(mine, feature // 2, 0, keepdims=False)
        got = lax.dynamic_index_in_dim(other, feature // 2, 0, keepdims=False)
        blocks.append(jnp.where(feature % 2 == core, own, got))
    return blocks


def halve(value, bit, swap):
    length = value.shape[0] // 2
    kept = lax.dynamic_slice_in_dim(value, bit * length, length, 0)
    given = lax.dynamic_slice_in_dim(value, (1 - bit) * length, length, 0)
    return kept + swap(given)


def double_factor(value, bit, swap):
    got = swap(value)
    return jnp.concatenate([jnp.where(bit == 0, value, got), jnp.where(bit == 0, got, value)])


def spread_right(factor, place):
    plane, y, core, x = place
    rows = factor.shape[0]
    value = factor.astype(BF16)
    kept = lax.dynamic_slice_in_dim(value, (y % 2) * 2 * rows, 2 * rows, 1)
    given = lax.dynamic_slice_in_dim(value, (1 - y % 2) * 2 * rows, 2 * rows, 1)
    got = flip_y(given, 1)
    low = y % 2 == 0
    pair = jnp.stack([jnp.where(low, kept, got), jnp.where(low, got, kept)])
    other = flip_core(pair)
    first = core == 0
    blocks = jnp.concatenate([jnp.where(first, pair, other), jnp.where(first, other, pair)])
    return rolled(blocks, y).reshape(ROWS * rows, 2 * rows)


def reduce_gradient(block_for, beside):
    halves = lambda value: jnp.split(value, 2)
    far = halves(block_for(PLANES // 2))
    running = {(0, 1): far[0], (1, -1): far[1]}
    for step in range(1, PLANES // 2 + 1):
        for stream in (0, 1):
            for way in (1, -1):
                if (stream, way) in running:
                    running[stream, way] = push_z(running[stream, way], way)
        left = PLANES // 2 - step
        if left == 1:
            running[0, 1], *beside = tie(running[0, 1], *beside)
        if left > 0:
            for way in (1, -1):
                for stream, own in enumerate(halves(block_for(way * left))):
                    value = running.get((stream, way))
                    running[stream, way] = own if value is None else own + value
    own = halves(block_for(0))
    sums = []
    for stream in (0, 1):
        value = own[stream].astype(F32) + running[stream, 1].astype(F32)
        sums.append(value + running[stream, -1].astype(F32))
    return jnp.concatenate(sums), beside


def body(tokens, weight, out_grad, owner_index, input_factor, output_factor):
    section, rank, x = (lax.axis_index(name) for name in AXES)
    half, y, core = rank // (ROWS * CORES), rank // CORES % ROWS, rank % CORES
    plane = half * SECTIONS + section
    place = (plane, y, core, x)
    width = weight.shape[2]
    share = tokens.shape[0] // SECTIONS
    total_tokens = tokens.shape[0] * HALVES * ROWS * CORES

    low = lambda value: flip_y(value, 1)
    high = lambda value: flip_y(value, 2)

    streams = swap_weight(weight[0], place)
    streams[0], input_factor = tie(streams[0], input_factor)

    token_share = lax.dynamic_slice_in_dim(tokens, section * share, share, 0)
    grad_share = lax.dynamic_slice_in_dim(out_grad, section * share, share, 0)
    pieces = []
    for mask in range(ROWS):
        part = quarter(grad_share, y ^ mask)
        both = jnp.concatenate([token_share, part], axis=1)
        pieces.append(flip_y(both, mask) if mask else both)
    both = natural(pieces, y, 0)
    full, cotangent = both[:, : ROWS * width], both[:, ROWS * width :]
    flowing = quarter(full, y)

    factor = input_factor[0, 0].astype(BF16)
    factor = jnp.where(rank == owner_index[0], factor, jnp.zeros_like(factor))
    factor = halve(factor, core, flip_core)
    beside = (full, flowing, cotangent, factor)
    held, (full, flowing, cotangent, factor) = gather_weight(streams, place, beside)
    weights = [section_weight(held, s, place) for s in range(SECTIONS)]

    factor = halve(factor, y % 2, low)
    inputs, hiddens = [], []
    for s in range(SECTIONS):
        inputs.append(full)
        parts = [product(full, weights[s][k]) for k in range(COLUMNS)]
        hidden = parts[0]
        for k in range(1, COLUMNS):
            hidden = hidden + push_x(parts[k].astype(BF16), k).astype(F32)
        if s == 1:
            factor = halve(factor, y // 2, high)
        elif s == 3:
            factor = double_factor(factor, y // 2, high)
        if s != 2:
            hidden, factor = tie(hidden, factor)
        hiddens.append(hidden)
        if s == 1:
            factor = factor + push_z(factor, PLANES // 2)
        if s + 1 < SECTIONS:
            flowing = (flowing.astype(F32) + activate(hidden)).astype(BF16)
            pieces = [flowing] + [flip_y(flowing, mask) for mask in range(1, ROWS)]
            full = natural(pieces, y, 1)
        if s in (0, 2):
            full, factor = tie(full, factor)

    inputs = jnp.stack(inputs)
    inputs = jnp.concatenate([inputs, flip_core(inputs)], axis=1)

    grads = [None] * SECTIONS
    for s in reversed(range(SECTIONS)):
        local_grad = gelu_back(hiddens[s], cotangent.astype(F32)).astype(BF16)
        grad = [local_grad] + [push_x(local_grad, -k) for k in range(1, COLUMNS)]
        if s == 3:
            factor = double_factor(factor, y % 2, low)
            grad[1], factor = tie(grad[1], factor)
            factor = double_factor(factor, core, flip_core)
        grads[s] = rolled(jnp.stack(grad), (COLUMNS - x) % COLUMNS)
        if s > 0:
            passed = sum(product(grad[k], weights[s][k], 1, 1) for k in range(COLUMNS))
            new = cotangent.astype(F32) + quarter(passed, y)
            for mask in range(1, ROWS):
                sent = quarter(passed, y ^ mask).astype(BF16)
                new = new + flip_y(sent, mask).astype(F32)
            cotangent = new.astype(BF16)
        if s == 1:
            cotangent, inputs, factor = tie(cotangent, inputs, factor)

    grads = jnp.stack(grads)
    grads = grads.reshape(SECTIONS, HALVES, CORES, *local_grad.shape)
    kept = lax.dynamic_index_in_dim(grads, core, 2, keepdims=False)
    given = lax.dynamic_index_in_dim(grads, 1 - core, 2, keepdims=False)
    grads = jnp.concatenate([kept, flip_core(given)], axis=2)

    def block_for(distance):
        aim = (plane + distance) % PLANES
        at, which = aim % SECTIONS, aim // SECTIONS
        chosen = lax.dynamic_index_in_dim(inputs, at, 0, keepdims=False)
        grad = lax.dynamic_slice(grads, (at, which, 0, 0), (1, 1) + grads.shape[2:])[0, 0]
        return product(chosen, grad, 0, 0).astype(BF16)

    right = spread_right(output_factor[0], place)
    gradient, (factor, right) = reduce_gradient(block_for, (factor, right))
    gradient = (gradient / total_tokens).astype(BF16)
    left = product(factor, gradient).astype(BF16)

    def to_user(by):
        def to(z, y, c, x):
            there = (y + by) % ROWS
            return (z, there, c, x) if there // 2 == c else None

        return to

    near, far = jnp.split(left, 2)

    def halfway(z, y, c, x):
        return (z, (y - 1) % ROWS, c, x) if (y - 2) % ROWS // 2 == c else None

    far = move(move(far, halfway), to_user(-1))
    pieces = [left, move(left, to_user(-1)), None, move(left, to_user(1))]
    pieces[2] = jnp.concatenate([move(near, to_user(2)), far])
    both = product(jnp.concatenate(pieces, axis=1), right)
    kept = lax.dynamic_slice_in_dim(both, core * width, width, 1)
    given = lax.dynamic_slice_in_dim(both, (1 - core) * width, width, 1).astype(BF16)
    got = move(given, lambda z, y, c, x: (z, y, 1 - c, x) if y // 2 == c else None)
    result = jnp.where(y // 2 == core, kept, got.astype(F32))
    return result[None]


def solution(mesh):
    placed = (
        P("dp", "tensor"),
        P("section", "tensor", "dp"),
        P("dp", "tensor"),
        P("section"),
        P("section", "dp", "tensor", None),
        P("section", "dp", None),
    )
    return jax.shard_map(
        body, mesh=mesh, in_specs=placed, out_specs=P("section", "tensor", "dp"), check_vma=False
    )
```

```python
import jax
import jax.numpy as jnp
from jax import lax
from jax.sharding import PartitionSpec as P

AXES = ("section", "dp", "tensor")
SECTIONS, HALVES, ROWS, CORES, COLUMNS = 4, 2, 4, 2, 4
PLANES = HALVES * SECTIONS
F32, BF16 = jnp.float32, jnp.bfloat16


def number(plane, y, core, x):
    half, section = plane // SECTIONS, plane % SECTIONS
    return (section * HALVES * ROWS * CORES + (half * ROWS + y) * CORES + core) * COLUMNS + x


def move(block, to):
    route = []
    for plane in range(PLANES):
        for y in range(ROWS):
            for core in range(CORES):
                for x in range(COLUMNS):
                    there = to(plane, y, core, x)
                    if there is not None:
                        route.append((number(plane, y, core, x), number(*there)))
    return lax.ppermute(block, AXES, route)


def push_z(block, by):
    return move(block, lambda z, y, c, x: ((z + by) % PLANES, y, c, x))


def push_y(block, by):
    return move(block, lambda z, y, c, x: (z, (y + by) % ROWS, c, x))


def push_x(block, by):
    return move(block, lambda z, y, c, x: (z, y, c, (x + by) % COLUMNS))


def flip_core(block):
    return move(block, lambda z, y, c, x: (z, y, 1 - c, x))


def rolled(blocks, start):
    twice = jnp.concatenate([blocks, blocks])
    return lax.dynamic_slice_in_dim(twice, start, blocks.shape[0], 0)


def natural(pieces, y):
    blocks = rolled(jnp.stack(pieces), (ROWS - y) % ROWS)
    return jnp.concatenate([blocks[0], blocks[2], blocks[1], blocks[3]], axis=1)


def quarter(values, chip):
    size = values.shape[1] // ROWS
    return lax.dynamic_slice_in_dim(values, (chip % 2 * 2 + chip // 2) * size, size, 1)


def tie(*values):
    return lax.optimization_barrier(values)


def activate(values):
    return jax.nn.gelu(values, approximate=True)


def gelu_back(hidden, cotangent):
    return jax.vjp(activate, hidden)[1](cotangent)[0]


def product(left, right, left_dim=1, right_dim=0):
    return lax.dot_general(
        left, right, (((left_dim,), (right_dim,)), ((), ())), preferred_element_type=F32
    )


def swap_weight(weight, place):
    plane, y, core, x = place
    swap = lambda z, y, c, x: (z, 2 * c + y % 2, y // 2, x) if y // 2 != c else None
    streams = jnp.split(weight, 2)
    return [jnp.where(y // 2 == core, part, move(part, swap)) for part in streams]


def gather_weight(streams, place, beside):
    plane, y, core, x = place
    rows, cols = streams[0].shape
    held = jnp.zeros((PLANES, 2, rows, cols), streams[0].dtype)

    def put(held, block, stream, distance):
        at = ((plane + distance) % PLANES, stream, 0, 0)
        return lax.dynamic_update_slice(held, block[None, None], at)

    for stream in (0, 1):
        held = put(held, streams[stream], stream, 0)
    up, down = list(streams), list(streams)
    value = beside[0](None)
    for step in range(1, PLANES // 2 + 1):
        if step in (2, 4):
            down[1], value = tie(down[1], value)
            value = beside[step // 2](value)
        for stream in (0, 1):
            if step < PLANES // 2 or stream == 0:
                up[stream] = push_z(up[stream], 1)
                held = put(held, up[stream], stream, -step)
            if step < PLANES // 2 or stream == 1:
                down[stream] = push_z(down[stream], -1)
                held = put(held, down[stream], stream, step)
    return held.reshape(HALVES, SECTIONS, 2 * rows, cols), value


def section_weight(held, section, place):
    plane, y, core, x = place
    mine = held[:, section]
    other = flip_core(mine)
    blocks = []
    for k in range(COLUMNS):
        feature = (x + k) % COLUMNS
        own = lax.dynamic_index_in_dim(mine, feature // 2, 0, keepdims=False)
        got = lax.dynamic_index_in_dim(other, feature // 2, 0, keepdims=False)
        blocks.append(jnp.where(feature % 2 == core, own, got))
    return blocks


def flip_low(block):
    return move(block, lambda z, y, c, x: (z, y ^ 1, c, x))


def flip_high(block):
    return move(block, lambda z, y, c, x: (z, y ^ 2, c, x))


def halve(value, bit, swap):
    length = value.shape[0] // 2
    kept = lax.dynamic_slice_in_dim(value, bit * length, length, 0)
    given = lax.dynamic_slice_in_dim(value, (1 - bit) * length, length, 0)
    return kept + swap(given)


def double_factor(value, bit, swap):
    got = swap(value)
    return jnp.concatenate([jnp.where(bit == 0, value, got), jnp.where(bit == 0, got, value)])


def spread_right(factor, place):
    plane, y, core, x = place
    rows = factor.shape[0]
    value = factor.astype(BF16)
    kept = lax.dynamic_slice_in_dim(value, (y % 2) * 2 * rows, 2 * rows, 1)
    given = lax.dynamic_slice_in_dim(value, (1 - y % 2) * 2 * rows, 2 * rows, 1)
    got = flip_low(given)
    low = y % 2 == 0
    pair = jnp.stack([jnp.where(low, kept, got), jnp.where(low, got, kept)])
    other = flip_core(pair)
    first = core == 0
    blocks = jnp.concatenate([jnp.where(first, pair, other), jnp.where(first, other, pair)])
    return rolled(blocks, y).reshape(ROWS * rows, 2 * rows)


def reduce_gradient(block_for, beside):
    halves = lambda value: jnp.split(value, 2)
    far = halves(block_for(PLANES // 2))
    running = {(0, 1): far[0], (1, -1): far[1]}
    for step in range(1, PLANES // 2 + 1):
        for stream in (0, 1):
            for way in (1, -1):
                if (stream, way) in running:
                    running[stream, way] = push_z(running[stream, way], way)
        left = PLANES // 2 - step
        if left == 1:
            running[0, 1], *beside = tie(running[0, 1], *beside)
        if left > 0:
            for way in (1, -1):
                for stream, own in enumerate(halves(block_for(way * left))):
                    value = running.get((stream, way))
                    running[stream, way] = own if value is None else own + value
    own = halves(block_for(0))
    sums = []
    for stream in (0, 1):
        value = own[stream].astype(F32) + running[stream, 1].astype(F32)
        sums.append(value + running[stream, -1].astype(F32))
    return jnp.concatenate(sums), beside


def body(tokens, weight, out_grad, owner_index, input_factor, output_factor):
    section, rank, x = (lax.axis_index(name) for name in AXES)
    half, y, core = rank // (ROWS * CORES), rank // CORES % ROWS, rank % CORES
    plane = half * SECTIONS + section
    place = (plane, y, core, x)
    width = weight.shape[2]
    share = tokens.shape[0] // SECTIONS
    total_tokens = tokens.shape[0] * HALVES * ROWS * CORES

    streams = swap_weight(weight[0], place)

    def owned(unused):
        factor = input_factor[0, 0].astype(BF16)
        value = jnp.where(rank == owner_index[0], factor, jnp.zeros_like(factor))
        return halve(value, core, flip_core)

    steps = (
        owned,
        lambda value: halve(value, y % 2, flip_low),
        lambda value: halve(value, y // 2, flip_high),
    )
    held, factor = gather_weight(streams, place, steps)

    token_share = lax.dynamic_slice_in_dim(tokens, section * share, share, 0)
    grad_share = lax.dynamic_slice_in_dim(out_grad, section * share, share, 0)
    pieces = []
    for k in range(ROWS):
        part = quarter(grad_share, (y + ROWS - k) % ROWS)
        both = jnp.concatenate([token_share, part], axis=1)
        pieces.append(push_y(both, -k) if k else both)
    both = rolled(jnp.stack(pieces), (ROWS - y) % ROWS).reshape(ROWS * share, -1)
    full, cotangent = both[:, : ROWS * width], both[:, ROWS * width :]
    flowing = quarter(full, y)

    weights = [section_weight(held, s, place) for s in range(SECTIONS)]

    inputs, hiddens = [], []
    for s in range(SECTIONS):
        inputs.append(full)
        parts = [product(full, weights[s][k]) for k in range(COLUMNS)]
        hidden = parts[0]
        for k in range(1, COLUMNS):
            hidden = hidden + push_x(parts[k].astype(BF16), k).astype(F32)
        if s == 0:
            hidden, factor = tie(hidden, factor)
            factor = factor + push_z(factor, PLANES // 2)
        hiddens.append(hidden)
        if s + 1 < SECTIONS:
            flowing = (flowing.astype(F32) + activate(hidden)).astype(BF16)
            full = natural([flowing] + [push_y(flowing, -k) for k in range(1, ROWS)], y)
        if s == 2:
            full, factor = tie(full, factor)

    inputs = jnp.stack(inputs)
    inputs = jnp.concatenate([inputs, flip_core(inputs)], axis=1)

    grads = [None] * SECTIONS
    for s in reversed(range(SECTIONS)):
        local_grad = gelu_back(hiddens[s], cotangent.astype(F32)).astype(BF16)
        grad = [local_grad] + [push_x(local_grad, -k) for k in range(1, COLUMNS)]
        grads[s] = rolled(jnp.stack(grad), (COLUMNS - x) % COLUMNS)
        if s > 0:
            passed = sum(product(grad[k], weights[s][k], 1, 1) for k in range(COLUMNS))
            new = cotangent.astype(F32) + quarter(passed, y)
            for k in range(1, ROWS):
                sent = quarter(passed, (y + k) % ROWS).astype(BF16)
                new = new + push_y(sent, k).astype(F32)
            cotangent = new.astype(BF16)
        if s == 1:
            cotangent, inputs = tie(cotangent, inputs)

    grads = jnp.stack(grads)
    grads = grads.reshape(SECTIONS, HALVES, CORES, *local_grad.shape)
    kept = lax.dynamic_index_in_dim(grads, core, 2, keepdims=False)
    given = lax.dynamic_index_in_dim(grads, 1 - core, 2, keepdims=False)
    grads = jnp.concatenate([kept, flip_core(given)], axis=2)

    def block_for(distance):
        aim = (plane + distance) % PLANES
        at, which = aim % SECTIONS, aim // SECTIONS
        chosen = lax.dynamic_index_in_dim(inputs, at, 0, keepdims=False)
        grad = lax.dynamic_slice(grads, (at, which, 0, 0), (1, 1) + grads.shape[2:])[0, 0]
        return product(chosen, grad, 0, 0).astype(BF16)

    for bit, swap in ((y // 2, flip_high), (y % 2, flip_low), (core, flip_core)):
        factor = double_factor(factor, bit, swap)
    right = spread_right(output_factor[0], place)
    gradient, (factor, right) = reduce_gradient(block_for, (factor, right))
    gradient = (gradient / total_tokens).astype(BF16)
    left = product(factor, gradient).astype(BF16)

    def to_user(by):
        def to(z, y, c, x):
            there = (y + by) % ROWS
            return (z, there, c, x) if there // 2 == c else None

        return to

    near, far = jnp.split(left, 2)

    def halfway(z, y, c, x):
        return (z, (y - 1) % ROWS, c, x) if (y - 2) % ROWS // 2 == c else None

    far = move(move(far, halfway), to_user(-1))
    pieces = [left, move(left, to_user(-1)), None, move(left, to_user(1))]
    pieces[2] = jnp.concatenate([move(near, to_user(2)), far])
    both = product(jnp.concatenate(pieces, axis=1), right)
    kept = lax.dynamic_slice_in_dim(both, core * width, width, 1)
    given = lax.dynamic_slice_in_dim(both, (1 - core) * width, width, 1).astype(BF16)
    got = move(given, lambda z, y, c, x: (z, y, 1 - c, x) if y // 2 == c else None)
    result = jnp.where(y // 2 == core, kept, got.astype(F32))
    return result[None]


def solution(mesh):
    placed = (
        P("dp", "tensor"),
        P("section", "tensor", "dp"),
        P("dp", "tensor"),
        P("section"),
        P("section", "dp", "tensor", None),
        P("section", "dp", None),
    )
    return jax.shard_map(
        body, mesh=mesh, in_specs=placed, out_specs=P("section", "tensor", "dp"), check_vma=False
    )
```

```python
import jax
import jax.numpy as jnp
from jax import lax
from jax.sharding import PartitionSpec as P

AXES = ("section", "dp", "tensor")
SECTIONS, HALVES, ROWS, CORES, COLUMNS = 4, 2, 4, 2, 4
PLANES = HALVES * SECTIONS
F32, BF16 = jnp.float32, jnp.bfloat16


def number(plane, y, core, x):
    half, section = plane // SECTIONS, plane % SECTIONS
    return (section * HALVES * ROWS * CORES + (half * ROWS + y) * CORES + core) * COLUMNS + x


def move(block, to):
    route = []
    for plane in range(PLANES):
        for y in range(ROWS):
            for core in range(CORES):
                for x in range(COLUMNS):
                    there = to(plane, y, core, x)
                    if there is not None:
                        route.append((number(plane, y, core, x), number(*there)))
    return lax.ppermute(block, AXES, route)


def push_z(block, by):
    return move(block, lambda z, y, c, x: ((z + by) % PLANES, y, c, x))


def push_y(block, by):
    return move(block, lambda z, y, c, x: (z, (y + by) % ROWS, c, x))


def push_x(block, by):
    return move(block, lambda z, y, c, x: (z, y, c, (x + by) % COLUMNS))


def flip_core(block):
    return move(block, lambda z, y, c, x: (z, y, 1 - c, x))


def rolled(blocks, start):
    twice = jnp.concatenate([blocks, blocks])
    return lax.dynamic_slice_in_dim(twice, start, blocks.shape[0], 0)


def natural(pieces, y):
    blocks = rolled(jnp.stack(pieces), (ROWS - y) % ROWS)
    return jnp.concatenate([blocks[0], blocks[2], blocks[1], blocks[3]], axis=1)


def quarter(values, chip):
    size = values.shape[1] // ROWS
    return lax.dynamic_slice_in_dim(values, (chip % 2 * 2 + chip // 2) * size, size, 1)


def tie(*values):
    return lax.optimization_barrier(values)


def activate(values):
    return jax.nn.gelu(values, approximate=True)


def gelu_back(hidden, cotangent):
    return jax.vjp(activate, hidden)[1](cotangent)[0]


def product(left, right, left_dim=1, right_dim=0):
    return lax.dot_general(
        left, right, (((left_dim,), (right_dim,)), ((), ())), preferred_element_type=F32
    )


def swap_weight(weight, place):
    plane, y, core, x = place
    swap = lambda z, y, c, x: (z, 2 * c + y % 2, y // 2, x) if y // 2 != c else None
    streams = jnp.split(weight, 2)
    return [jnp.where(y // 2 == core, part, move(part, swap)) for part in streams]


def gather_weight(streams, place, beside):
    plane, y, core, x = place
    rows, cols = streams[0].shape
    held = jnp.zeros((PLANES, 2, rows, cols), streams[0].dtype)

    def put(held, block, stream, distance):
        at = ((plane + distance) % PLANES, stream, 0, 0)
        return lax.dynamic_update_slice(held, block[None, None], at)

    for stream in (0, 1):
        held = put(held, streams[stream], stream, 0)
    up, down = list(streams), list(streams)
    value = None
    for step in range(1, PLANES // 2 + 1):
        if step in (2, 4):
            down[1], value = tie(down[1], value)
        if step != 3:
            value = beside[step // 2](value)
        for stream in (0, 1):
            if step < PLANES // 2 or stream == 0:
                up[stream] = push_z(up[stream], 1)
                held = put(held, up[stream], stream, -step)
            if step < PLANES // 2 or stream == 1:
                down[stream] = push_z(down[stream], -1)
                held = put(held, down[stream], stream, step)
    return held.reshape(HALVES, SECTIONS, 2 * rows, cols), value


def section_weight(held, section, place):
    plane, y, core, x = place
    mine = held[:, section]
    other = flip_core(mine)
    blocks = []
    for k in range(COLUMNS):
        feature = (x + k) % COLUMNS
        own = lax.dynamic_index_in_dim(mine, feature // 2, 0, keepdims=False)
        got = lax.dynamic_index_in_dim(other, feature // 2, 0, keepdims=False)
        blocks.append(jnp.where(feature % 2 == core, own, got))
    return blocks


def flip_low(block):
    return move(block, lambda z, y, c, x: (z, y ^ 1, c, x))


def flip_high(block):
    return move(block, lambda z, y, c, x: (z, y ^ 2, c, x))


def halve(value, bit, swap):
    length = value.shape[0] // 2
    kept = lax.dynamic_slice_in_dim(value, bit * length, length, 0)
    given = lax.dynamic_slice_in_dim(value, (1 - bit) * length, length, 0)
    return kept + swap(given)


def double_factor(value, bit, swap):
    got = swap(value)
    return jnp.concatenate([jnp.where(bit == 0, value, got), jnp.where(bit == 0, got, value)])


def spread_right(factor, place):
    plane, y, core, x = place
    rows = factor.shape[0]
    value = factor.astype(BF16)
    kept = lax.dynamic_slice_in_dim(value, (y % 2) * 2 * rows, 2 * rows, 1)
    given = lax.dynamic_slice_in_dim(value, (1 - y % 2) * 2 * rows, 2 * rows, 1)
    got = flip_low(given)
    low = y % 2 == 0
    pair = jnp.stack([jnp.where(low, kept, got), jnp.where(low, got, kept)])
    other = flip_core(pair)
    first = core == 0
    blocks = jnp.concatenate([jnp.where(first, pair, other), jnp.where(first, other, pair)])
    return rolled(blocks, y).reshape(ROWS * rows, 2 * rows)


def reduce_gradient(block_for, beside):
    halves = lambda value: jnp.split(value, 2)
    far = halves(block_for(PLANES // 2))
    running = {(0, 1): far[0], (1, -1): far[1]}
    for step in range(1, PLANES // 2 + 1):
        for stream in (0, 1):
            for way in (1, -1):
                if (stream, way) in running:
                    running[stream, way] = push_z(running[stream, way], way)
        left = PLANES // 2 - step
        if left == 1:
            running[0, 1], *beside = tie(running[0, 1], *beside)
        if left > 0:
            for way in (1, -1):
                for stream, own in enumerate(halves(block_for(way * left))):
                    value = running.get((stream, way))
                    running[stream, way] = own if value is None else own + value
    own = halves(block_for(0))
    sums = []
    for stream in (0, 1):
        value = own[stream].astype(F32) + running[stream, 1].astype(F32)
        sums.append(value + running[stream, -1].astype(F32))
    return jnp.concatenate(sums), beside


def body(tokens, weight, out_grad, owner_index, input_factor, output_factor):
    section, rank, x = (lax.axis_index(name) for name in AXES)
    half, y, core = rank // (ROWS * CORES), rank // CORES % ROWS, rank % CORES
    plane = half * SECTIONS + section
    place = (plane, y, core, x)
    width = weight.shape[2]
    share = tokens.shape[0] // SECTIONS
    total_tokens = tokens.shape[0] * HALVES * ROWS * CORES

    streams = swap_weight(weight[0], place)
    streams[0], input_factor = tie(streams[0], input_factor)

    def owned(unused):
        factor = input_factor[0, 0].astype(BF16)
        value = jnp.where(rank == owner_index[0], factor, jnp.zeros_like(factor))
        return halve(value, core, flip_core)

    steps = (
        owned,
        lambda value: halve(value, y % 2, flip_low),
        lambda value: halve(value, y // 2, flip_high),
    )
    held, factor = gather_weight(streams, place, steps)

    token_share = lax.dynamic_slice_in_dim(tokens, section * share, share, 0)
    grad_share = lax.dynamic_slice_in_dim(out_grad, section * share, share, 0)
    pieces = []
    for k in range(ROWS):
        part = quarter(grad_share, (y + ROWS - k) % ROWS)
        both = jnp.concatenate([token_share, part], axis=1)
        pieces.append(push_y(both, -k) if k else both)
    both = rolled(jnp.stack(pieces), (ROWS - y) % ROWS).reshape(ROWS * share, -1)
    full, cotangent = both[:, : ROWS * width], both[:, ROWS * width :]
    flowing = quarter(full, y)

    weights = [section_weight(held, s, place) for s in range(SECTIONS)]
    factor = factor + push_z(factor, PLANES // 2)

    inputs, hiddens = [], []
    for s in range(SECTIONS):
        inputs.append(full)
        parts = [product(full, weights[s][k]) for k in range(COLUMNS)]
        hidden = parts[0]
        for k in range(1, COLUMNS):
            hidden = hidden + push_x(parts[k].astype(BF16), k).astype(F32)
        hiddens.append(hidden)
        if s + 1 < SECTIONS:
            flowing = (flowing.astype(F32) + activate(hidden)).astype(BF16)
            full = natural([flowing] + [push_y(flowing, -k) for k in range(1, ROWS)], y)
        if s == 2:
            full, factor = tie(full, factor)

    inputs = jnp.stack(inputs)
    inputs = jnp.concatenate([inputs, flip_core(inputs)], axis=1)

    grads = [None] * SECTIONS
    for s in reversed(range(SECTIONS)):
        local_grad = gelu_back(hiddens[s], cotangent.astype(F32)).astype(BF16)
        grad = [local_grad] + [push_x(local_grad, -k) for k in range(1, COLUMNS)]
        grads[s] = rolled(jnp.stack(grad), (COLUMNS - x) % COLUMNS)
        if s > 0:
            passed = sum(product(grad[k], weights[s][k], 1, 1) for k in range(COLUMNS))
            new = cotangent.astype(F32) + quarter(passed, y)
            for k in range(1, ROWS):
                sent = quarter(passed, (y + k) % ROWS).astype(BF16)
                new = new + push_y(sent, k).astype(F32)
            cotangent = new.astype(BF16)
        if s == 1:
            cotangent, inputs = tie(cotangent, inputs)

    grads = jnp.stack(grads)
    grads = grads.reshape(SECTIONS, HALVES, CORES, *local_grad.shape)
    kept = lax.dynamic_index_in_dim(grads, core, 2, keepdims=False)
    given = lax.dynamic_index_in_dim(grads, 1 - core, 2, keepdims=False)
    grads = jnp.concatenate([kept, flip_core(given)], axis=2)

    def block_for(distance):
        aim = (plane + distance) % PLANES
        at, which = aim % SECTIONS, aim // SECTIONS
        chosen = lax.dynamic_index_in_dim(inputs, at, 0, keepdims=False)
        grad = lax.dynamic_slice(grads, (at, which, 0, 0), (1, 1) + grads.shape[2:])[0, 0]
        return product(chosen, grad, 0, 0).astype(BF16)

    for bit, swap in ((y // 2, flip_high), (y % 2, flip_low), (core, flip_core)):
        factor = double_factor(factor, bit, swap)
    right = spread_right(output_factor[0], place)
    gradient, (factor, right) = reduce_gradient(block_for, (factor, right))
    gradient = (gradient / total_tokens).astype(BF16)
    left = product(factor, gradient).astype(BF16)

    def to_user(by):
        def to(z, y, c, x):
            there = (y + by) % ROWS
            return (z, there, c, x) if there // 2 == c else None

        return to

    near, far = jnp.split(left, 2)

    def halfway(z, y, c, x):
        return (z, (y - 1) % ROWS, c, x) if (y - 2) % ROWS // 2 == c else None

    far = move(move(far, halfway), to_user(-1))
    pieces = [left, move(left, to_user(-1)), None, move(left, to_user(1))]
    pieces[2] = jnp.concatenate([move(near, to_user(2)), far])
    both = product(jnp.concatenate(pieces, axis=1), right)
    kept = lax.dynamic_slice_in_dim(both, core * width, width, 1)
    given = lax.dynamic_slice_in_dim(both, (1 - core) * width, width, 1).astype(BF16)
    got = move(given, lambda z, y, c, x: (z, y, 1 - c, x) if y // 2 == c else None)
    result = jnp.where(y // 2 == core, kept, got.astype(F32))
    return result[None]


def solution(mesh):
    placed = (
        P("dp", "tensor"),
        P("section", "tensor", "dp"),
        P("dp", "tensor"),
        P("section"),
        P("section", "dp", "tensor", None),
        P("section", "dp", None),
    )
    return jax.shard_map(
        body, mesh=mesh, in_specs=placed, out_specs=P("section", "tensor", "dp"), check_vma=False
    )
```
